256 devices in a mesh: head: 4 (over z_hi), ctx: 64 (over z_lo, y, x, core).
Axes of the slice: x: 4, y: 4, z: 8 (z_hi: 4, z_lo: 2; z = z_hi * 2 + z_lo), core: 2. Of those that a mesh axis runs over, the one named last changes fastest.
Arguments:
- query: bfloat16 [32768, 8192], P(('ctx', 'head')), may hold values from -6 to 6
- key: bfloat16 [32768, 1024], P(('ctx', 'head')), may hold values from -6 to 6
- value: bfloat16 [32768, 1024], P(('ctx', 'head')), may hold values from -6 to 6
- out: bfloat16 [32768, 8192], P(('ctx', 'head')), may hold values from -6 to 6
- dout: bfloat16 [32768, 8192], P(('ctx', 'head')), may hold values from -6 to 6
- lse: float32 [32768, 64], P('ctx', 'head'), may hold values from 3 to 6
- span_order: int32 [128], replicated, may hold values from 0 to 127, each once
Outputs:
- grad_query: bfloat16 [32768, 8192], P(('ctx', 'head'))
- grad_key: bfloat16 [32768, 1024], P(('ctx', 'head'))
- grad_value: bfloat16 [32768, 1024], P(('ctx', 'head'))
The draws below stay inside these ranges and needn't reach their ends.
Inputs may be any that keep to these rules, and one draw needn't show every extreme that they name: `span_order`: each of the 128 spans appears once.
All inputs are finite; a program needn't handle non-finite values.
Results may differ from the reference program's by a relative error of at most 0.0052.
Values may be sent and summed in bfloat16 or wider, within the bound.
A program may use at most 128 MiB of HBM per device.

```python
import jax
import jax.numpy as jnp
from jax import lax

HEADS = 64
KV_HEADS = 8
HD = 128
TOK_DEV = 512
STEPS = 2
TOKENS = 32768
N_CTX = 64


def level_of(own_key, dims, shards, low, high):
    def one(position, blocks):
        draws = jax.random.uniform(jax.random.fold_in(jax.random.fold_in(own_key, 6), position), (blocks,), jnp.float32, low / len(shards), high / len(shards))
        return jnp.repeat(jnp.exp(draws), dims[position] // blocks).reshape((-1,) + (1,) * (len(dims) - position - 1))

    level = one(*shards[0])
    for cut in shards[1:]:
        level = level * one(*cut)
    return level


def centred(own_key, extent, spread, bound, shards=(), held_as=jnp.bfloat16):
    values = jax.random.normal(own_key, extent, jnp.float32) * spread
    if len(shards) > 0:
        values = level_of(own_key, extent, shards, -0.22, 0.18) * values
    return jnp.clip(values, min=-bound, max=bound).astype(held_as)


def setup_inputs(seed: int = 0) -> dict:
    key_list = jax.random.split(jax.random.key(seed), 8)
    return {
        "query": centred(key_list[0], (TOKENS, HEADS * HD), 1.0, 6.0, ((0, 256),)),
        "key": centred(key_list[1], (TOKENS, KV_HEADS * HD), 1.0, 6.0, ((0, 256),)),
        "value": centred(key_list[2], (TOKENS, KV_HEADS * HD), 1.0, 6.0, ((0, 256),)),
        "out": centred(key_list[3], (TOKENS, HEADS * HD), 1.0, 6.0, ((0, 256),)),
        "dout": centred(key_list[4], (TOKENS, HEADS * HD), 1.0, 6.0, ((0, 256),)),
        "lse": jnp.clip(3.0 + 3.0 * jax.random.uniform(key_list[5], (TOKENS, HEADS), jnp.float32) ** level_of(key_list[5], (TOKENS, HEADS), ((0, 64), (1, 4)), -0.2, 0.2), 3.0, 6.0),
        "span_order": jax.random.permutation(key_list[6], 2 * N_CTX).astype(jnp.int32),
    }


def span_positions(span_order, block, half_rows):
    pair = lax.dynamic_slice_in_dim(span_order, (2 * block).astype(jnp.int32), 2, 0)
    offsets = jnp.arange(half_rows, dtype=jnp.int32)
    return jnp.concatenate([pair[0] * half_rows + offsets, pair[1] * half_rows + offsets])


def pair_grads(query_b, dout_b, delta_b, lse_b, key_b, value_b, allowed, scale):
    rows, heads, width = query_b.shape
    groups = key_b.shape[1]
    per = heads // groups
    q_four = query_b.reshape(rows, groups, per, width).astype(jnp.float32)
    d_four = dout_b.reshape(rows, groups, per, width).astype(jnp.float32)
    key_f = key_b.astype(jnp.float32)
    value_f = value_b.astype(jnp.float32)
    scores = jnp.einsum("qgjd,kgd->gjqk", q_four, key_f) * scale
    offset = jnp.transpose(lse_b.reshape(rows, groups, per), (1, 2, 0))[..., None]
    probs = jnp.where(allowed, jnp.exp(scores - offset), jnp.float32(0.0))
    probs_low = probs.astype(jnp.bfloat16).astype(jnp.float32)
    grad_value = jnp.einsum("gjqk,qgjd->kgd", probs_low, d_four)
    grad_probs = jnp.einsum("qgjd,kgd->gjqk", d_four, value_f)
    base = jnp.transpose(delta_b.reshape(rows, groups, per), (1, 2, 0))[..., None]
    grad_scores = (probs * (grad_probs - base) * scale).astype(jnp.bfloat16).astype(jnp.float32)
    grad_query = jnp.einsum("gjqk,kgd->qgjd", grad_scores, key_f).reshape(rows, heads * width)
    grad_key = jnp.einsum("gjqk,qgjd->kgd", grad_scores, q_four).reshape(rows, groups * width)
    return grad_query, grad_key, grad_value.reshape(rows, groups * width)


def reference(query, key, value, out, dout, lse, span_order):
    rows = TOK_DEV
    half = rows // 2
    scale = HD ** -0.5
    delta = jnp.sum((out.astype(jnp.float32) * dout.astype(jnp.float32)).reshape(TOKENS, HEADS, HD), axis=2)
    q_blocks = query.reshape(N_CTX, rows, HEADS, HD)
    d_blocks = dout.reshape(N_CTX, rows, HEADS, HD)
    k_blocks = key.reshape(N_CTX, rows, KV_HEADS, HD)
    v_blocks = value.reshape(N_CTX, rows, KV_HEADS, HD)
    delta_blocks = delta.reshape(N_CTX, rows, HEADS)
    lse_blocks = lse.reshape(N_CTX, rows, HEADS)
    blocks = jnp.arange(N_CTX, dtype=jnp.int32)
    grad_q = jnp.zeros((N_CTX, rows, HEADS * HD), jnp.float32)
    grad_k = jnp.zeros((N_CTX, rows, KV_HEADS * HD), jnp.float32)
    grad_v = jnp.zeros((N_CTX, rows, KV_HEADS * HD), jnp.float32)
    for step in range(STEPS):
        def one_block(block):
            source = ((block - step) % N_CTX).astype(jnp.int32)
            own_pos = span_positions(span_order, block, half)
            key_pos = span_positions(span_order, source, half)
            allowed = own_pos[:, None] >= key_pos[None, :]
            return pair_grads(q_blocks[block], d_blocks[block], delta_blocks[block], lse_blocks[block],
                              k_blocks[source], v_blocks[source], allowed, scale)

        part_q, part_k, part_v = lax.map(one_block, blocks)
        grad_q = grad_q + part_q
        grad_k = grad_k + jnp.roll(part_k, -step, axis=0)
        grad_v = grad_v + jnp.roll(part_v, -step, axis=0)
    return (grad_q.reshape(TOKENS, HEADS * HD).astype(jnp.bfloat16),
            grad_k.reshape(TOKENS, KV_HEADS * HD).astype(jnp.bfloat16),
            grad_v.reshape(TOKENS, KV_HEADS * HD).astype(jnp.bfloat16))
```

```python
import functools
import math

import jax
import jax.numpy as jnp
from jax import lax
from jax.experimental import pallas as pl
from jax.experimental.pallas import tpu as pltpu
from jax.sharding import PartitionSpec as P

HD = 128
RING = 4
LOG2E = math.log2(math.e)
FAR = 1e30
AHEAD = 2
MESH = pl.DeviceIdType.MESH
NT = (((1,), (1,)), ((), ()))
NN = (((1,), (0,)), ((), ()))


def dot(a, b, dims):
    return lax.dot_general(a, b, dims, preferred_element_type=jnp.float32)


def kernel(
    groups, per, q_hbm, k_hbm, v_hbm, o_hbm, d_hbm, lse_hbm, span_ref,
    dq_hbm, dk_hbm, dv_hbm,
    q_buf, d_buf, o_buf, lse_buf, lse_cut, lse_all, delta_all, bias_own,
    kv, grad, back_out, back_in, cut_out, cut_in, sum_out, sum_in, dq_buf, dk_buf, dv_buf,
    load_sem, kv_sem, store_sem,
    lse_s, lse_r, own_s, own_r, fwd_s, fwd_r, ctx_s, ctx_r, back_s, back_r, cut_s, cut_r, sum_s, sum_r,
):
    rows = q_buf.shape[0]
    span = 2 * rows
    heads_in = lse_cut.shape[1]
    cycle = lax.axis_size("ctx")
    me = lax.axis_index("head")
    here = lax.axis_index("ctx")
    up, opp, dn = lax.rem(me + 1, RING), lax.rem(me + 2, RING), lax.rem(me + 3, RING)
    nx, pv = lax.rem(here + 1, cycle), lax.rem(here + cycle - 1, cycle)
    at_up, at_dn, at_opp = (up, here), (dn, here), (opp, here)
    at_nx, at_pv = (me, nx), (me, pv)
    scale = HD ** -0.5

    def lanes(g, width=HD):
        return pl.ds(pl.multiple_of(g * width, width), width)

    def load(i):
        src, dst = ((q_hbm, q_buf), (d_hbm, d_buf), (o_hbm, o_buf), (lse_hbm, lse_buf))[i]
        return pltpu.make_async_copy(src, dst, load_sem.at[i])

    def load_kv(which, g):
        src = (k_hbm, v_hbm)[which]
        return pltpu.make_async_copy(src.at[:, lanes(g)], kv.at[0, g, which, me], kv_sem.at[which, g])

    def remote(src, dst, s, r, to):
        return pltpu.make_async_remote_copy(
            src_ref=src, dst_ref=dst, send_sem=s, recv_sem=r, device_id=to, device_id_type=MESH
        )

    def send_lse(i):
        to, target = ((up, at_up), (dn, at_dn), (opp, at_opp))[i]
        return remote(lse_cut.at[to], lse_all.at[me], lse_s.at[i], lse_r.at[i], target)

    def take_lse(i):
        src = (dn, up, opp)[i]
        return remote(lse_cut.at[src], lse_all.at[src], lse_s.at[i], lse_r.at[i], at_up)

    def own(side, g, slot):
        block = kv.at[0, g, :, slot]
        return remote(block, block, own_s.at[side, g], own_r.at[side, g], (at_up, at_dn)[side])

    def fwd(side, g, slot):
        block = kv.at[0, g, side, slot]
        return remote(block, block, fwd_s.at[side, g], fwd_r.at[side, g], (at_up, at_dn)[side])

    def ctx(g):
        return remote(kv.at[0, g], kv.at[1, g], ctx_s.at[g], ctx_r.at[g], at_nx)

    def back(g):
        return remote(back_out.at[g], back_in.at[g], back_s.at[g], back_r.at[g], at_pv)

    def cut(side, g):
        return remote(
            cut_out.at[g, side], cut_in.at[g, side], cut_s.at[side, g], cut_r.at[side, g], (at_up, at_dn)[side]
        )

    def summed(side, g):
        return remote(
            sum_out.at[g, side], sum_in.at[g, side], sum_s.at[side, g], sum_r.at[side, g], (at_up, at_dn)[side]
        )

    def store(g):
        return pltpu.make_async_copy(
            dq_buf.at[:, lanes(g, per * HD)], dq_hbm.at[:, lanes(g, per * HD)], store_sem.at[g]
        )

    def loop(lo, hi, body):
        def step(i, carry):
            body(i)
            return carry

        lax.fori_loop(lo, hi, step, 0)

    def start_kv(g):
        load_kv(0, g).start()
        load_kv(1, g).start()

    loop(0, groups, start_kv)
    for i in (3, 1, 2, 0):
        load(i).start()

    barrier = pltpu.get_barrier_semaphore()
    for target in (at_up, at_dn, at_opp, at_nx, at_pv):
        pl.semaphore_signal(barrier, inc=1, device_id=target, device_id_type=MESH)

    span_q = span_ref[2 * here + me // 2]
    first_q = (me % 2) * rows
    row = lax.broadcasted_iota(jnp.int32, (span, 2 * rows), 0)
    lane = lax.broadcasted_iota(jnp.int32, (span, 2 * rows), 1)
    ahead = lax.rem(lane, rows) - row
    for a in range(2):
        least = (span_ref[2 * here + a] - span_q) * span - first_q
        bias_own[a] = jnp.where(ahead >= least, 0.0, FAR)
    bias_prev = [jnp.where(span_q > span_ref[2 * pv + a], 0.0, FAR) for a in range(2)]

    pl.semaphore_wait(barrier, 5)

    def send_own(g):
        load_kv(0, g).wait()
        load_kv(1, g).wait()
        own(0, g, me).start()
        own(1, g, me).start()

    loop(0, min(AHEAD, groups), send_own)

    load(3).wait()
    for h in range(RING):
        lse_cut[h] = lse_buf[pl.ds(h * rows, rows), :].T
    for i in range(3):
        send_lse(i).start()
    lse_all[me] = lse_cut[me]

    load(1).wait()
    load(2).wait()
    ones = jnp.ones((8, 2 * HD), jnp.bfloat16)

    def make_delta(h):
        prod = o_buf[:, lanes(h)].astype(jnp.float32) * d_buf[:, lanes(h)].astype(jnp.float32)
        high = prod.astype(jnp.bfloat16)
        low = (prod - high.astype(jnp.float32)).astype(jnp.bfloat16)
        delta_all[pl.ds(h, 1), :] = dot(ones, jnp.concatenate([high, low], axis=1), NT)[0:1]

    loop(0, groups * per, make_delta)
    load(0).wait()
    for i in range(3):
        take_lse(i).wait_recv()

    def compute(g):
        def pair(j, carry):
            head = g * per + 2 * j
            q_one, d_one = q_buf[:, lanes(head // 2, 2 * HD)], d_buf[:, lanes(head // 2, 2 * HD)]
            q2 = jnp.concatenate([q_one[:, :HD], q_one[:, HD:]], axis=0)
            d2 = jnp.concatenate([d_one[:, :HD], d_one[:, HD:]], axis=0)
            owner, low = head // heads_in, lax.rem(head, heads_in)
            lse2 = jnp.concatenate(
                [lse_all[owner, pl.ds(low, 1), :], lse_all[owner, pl.ds(low + 1, 1), :]], axis=1
            ) * LOG2E
            delta2 = jnp.concatenate([delta_all[pl.ds(head, 1), :], delta_all[pl.ds(head + 1, 1), :]], axis=1)
            dq_t = jnp.zeros((HD, 2 * rows), jnp.float32)
            for b in range(2):
                for a in range(2):
                    key = kv[b, g, 0, 2 * a : 2 * a + 2].reshape(span, HD)
                    value = kv[b, g, 1, 2 * a : 2 * a + 2].reshape(span, HD)
                    scores = dot(key, q2, NT) * (scale * LOG2E)
                    if b == 0:
                        scores = scores - lse2 - bias_own[a]
                    else:
                        scores = scores - (lse2 + bias_prev[a])
                    probs = jnp.exp2(scores)
                    grad_probs = dot(value, d2, NT)
                    grad_scores = (probs * (grad_probs - delta2) * scale).astype(jnp.bfloat16)
                    part_v = dot(probs.astype(jnp.bfloat16), d2, NN).reshape(2, rows, HD)
                    part_k = dot(grad_scores, q2, NN).reshape(2, rows, HD)
                    dq_t += dot(key.T, grad_scores, NN)
                    grad[g, b, 0, 2 * a : 2 * a + 2] += part_k
                    grad[g, b, 1, 2 * a : 2 * a + 2] += part_v
            dq_one = jnp.concatenate([dq_t[:, :rows].T, dq_t[:, rows:].T], axis=1)
            dq_buf[:, lanes(head // 2, 2 * HD)] = dq_one.astype(jnp.bfloat16)
            return carry

        grad[g] = jnp.zeros(grad.shape[1:], jnp.float32)
        lax.fori_loop(0, per // 2, pair, 0)
        back_out[g] = grad[g, 1].astype(jnp.bfloat16)

    def total(g, which, slot):
        return grad[g, 0, which, slot] + back_in[g, which, slot].astype(jnp.float32)

    def step(i):
        @pl.when(i < groups - AHEAD)
        def _():
            send_own(i + AHEAD)

        @pl.when(i < groups)
        def _():
            g = i
            own(0, g, dn).wait_recv()
            fwd(0, g, dn).start()
            own(1, g, up).wait_recv()
            fwd(1, g, up).start()

        @pl.when((i >= 1) & (i < groups + 1))
        def _():
            g = i - 1
            fwd(0, g, opp).wait_recv()
            fwd(1, g, opp).wait_recv()
            ctx(g).start()

        @pl.when((i >= 3) & (i < groups + 3))
        def _():
            g = i - 3
            back(g).wait_recv()
            cut_out[g, 0, 0] = total(g, 0, opp).astype(jnp.bfloat16)
            cut_out[g, 0, 1] = total(g, 1, up).astype(jnp.bfloat16)
            cut(0, g).start()
            cut_out[g, 1, 0] = total(g, 1, opp).astype(jnp.bfloat16)
            cut_out[g, 1, 1] = total(g, 0, dn).astype(jnp.bfloat16)
            cut(1, g).start()

        @pl.when((i >= 4) & (i < groups + 4))
        def _():
            g = i - 4
            cut(0, g).wait_recv()
            sum_out[g, 0] = (total(g, 0, up) + cut_in[g, 0, 0].astype(jnp.float32)).astype(jnp.bfloat16)
            summed(0, g).start()
            cut(1, g).wait_recv()
            sum_out[g, 1] = (total(g, 1, dn) + cut_in[g, 1, 0].astype(jnp.float32)).astype(jnp.bfloat16)
            summed(1, g).start()

        @pl.when((i >= 2) & (i < groups + 2))
        def _():
            g = i - 2
            ctx(g).wait_recv()
            compute(g)
            back(g).start()
            store(g).start()

        @pl.when(i >= 5)
        def _():
            g = i - 5
            summed(0, g).wait_recv()
            summed(1, g).wait_recv()
            for which, out in ((0, dk_buf), (1, dv_buf)):
                out[:, lanes(g)] = (
                    total(g, which, me)
                    + sum_in[g, which].astype(jnp.float32)
                    + cut_in[g, 1 - which, 1].astype(jnp.float32)
                ).astype(jnp.bfloat16)

    loop(0, groups + 5, step)

    last = [
        pltpu.make_async_copy(dk_buf, dk_hbm, load_sem.at[0]),
        pltpu.make_async_copy(dv_buf, dv_hbm, load_sem.at[1]),
    ]
    for copy in last:
        copy.start()

    def drain(g):
        for side in range(2):
            own(side, g, me).wait_send()
            fwd(side, g, (dn, up)[side]).wait_send()
            cut(side, g).wait_send()
            summed(side, g).wait_send()
        ctx(g).wait_send()
        back(g).wait_send()
        store(g).wait()

    loop(0, groups, drain)
    for i in range(3):
        send_lse(i).wait_send()
    for copy in last:
        copy.wait()


def body(query, key, value, out, dout, lse, span_order):
    rows, width = query.shape
    groups = key.shape[1] // HD
    per = width // key.shape[1]
    bf, f32 = jnp.bfloat16, jnp.float32
    dma = pltpu.SemaphoreType.DMA
    hbm = pl.BlockSpec(memory_space=pl.ANY)
    pairs = [dma((2, groups))] * 2
    ones = [dma((groups,))] * 2
    return pl.pallas_call(
        functools.partial(kernel, groups, per),
        out_shape=(
            jax.ShapeDtypeStruct(query.shape, bf),
            jax.ShapeDtypeStruct(key.shape, bf),
            jax.ShapeDtypeStruct(value.shape, bf),
        ),
        in_specs=[hbm] * 6 + [pl.BlockSpec(memory_space=pltpu.SMEM)],
        out_specs=[hbm] * 3,
        scratch_shapes=[
            pltpu.VMEM(query.shape, bf),
            pltpu.VMEM(query.shape, bf),
            pltpu.VMEM(query.shape, bf),
            pltpu.VMEM(lse.shape, f32),
            pltpu.VMEM((RING, lse.shape[1], rows), f32),
            pltpu.VMEM((RING, lse.shape[1], rows), f32),
            pltpu.VMEM((groups * per, rows), f32),
            pltpu.VMEM((2, 2 * rows, 2 * rows), f32),
            pltpu.VMEM((2, groups, 2, RING, rows, HD), bf),
            pltpu.VMEM((groups, 2, 2, RING, rows, HD), f32),
            pltpu.VMEM((groups, 2, RING, rows, HD), bf),
            pltpu.VMEM((groups, 2, RING, rows, HD), bf),
            pltpu.VMEM((groups, 2, 2, rows, HD), bf),
            pltpu.VMEM((groups, 2, 2, rows, HD), bf),
            pltpu.VMEM((groups, 2, rows, HD), bf),
            pltpu.VMEM((groups, 2, rows, HD), bf),
            pltpu.VMEM(query.shape, bf),
            pltpu.VMEM(key.shape, bf),
            pltpu.VMEM(value.shape, bf),
            dma((4,)),
            dma((2, groups)),
            dma((groups,)),
            dma((3,)),
            dma((3,)),
            *pairs,
            *pairs,
            *ones,
            *ones,
            *pairs,
            *pairs,
        ],
        compiler_params=pltpu.CompilerParams(
            collective_id=0, has_side_effects=True, vmem_limit_bytes=56 * 1024 * 1024
        ),
        cost_estimate=pl.CostEstimate(
            flops=20 * rows * width * RING * rows, bytes_accessed=10 * rows * width, transcendentals=0
        ),
    )(query, key, value, out, dout, lse, span_order)


def solution(mesh):
    token = P(("ctx", "head"), None)
    return jax.shard_map(
        body,
        mesh=mesh,
        in_specs=(token, token, token, token, token, P("ctx", "head"), P()),
        out_specs=(token, token, token),
        check_vma=False,
    )
```

```python
import functools
import math

import jax
import jax.numpy as jnp
from jax import lax
from jax.experimental import pallas as pl
from jax.experimental.pallas import tpu as pltpu
from jax.sharding import PartitionSpec as P

HD = 128
RING = 4
LOG2E = math.log2(math.e)
FAR = 1e30
AHEAD = 2
LAGS = (1, 3, 5, 6, 8)
MESH = pl.DeviceIdType.MESH
NT = (((1,), (1,)), ((), ()))
NN = (((1,), (0,)), ((), ()))


def dot(a, b, dims):
    return lax.dot_general(a, b, dims, preferred_element_type=jnp.float32)


def kernel(
    groups, per, q_hbm, k_hbm, v_hbm, o_hbm, d_hbm, lse_hbm, span_ref,
    dq_buf, dk_buf, dv_buf,
    q_buf, d_buf, o_buf, lse_buf, lse_cut, lse_all, delta_all, bias_own,
    kv, grad, back_out, back_in, cut_out, cut_in, sum_out, sum_in,
    key_t, p_all, s_all, q_all, d_all,
    load_sem, kv_sem,
    lse_s, lse_r, own_s, own_r, fwd_s, fwd_r, ctx_s, ctx_r, back_s, back_r, cut_s, cut_r, sum_s, sum_r,
):
    rows = q_buf.shape[0]
    span = 2 * rows
    heads_in = lse_cut.shape[1]
    cycle = lax.axis_size("ctx")
    me = lax.axis_index("head")
    here = lax.axis_index("ctx")
    up, opp, dn = lax.rem(me + 1, RING), lax.rem(me + 2, RING), lax.rem(me + 3, RING)
    nx, pv = lax.rem(here + 1, cycle), lax.rem(here + cycle - 1, cycle)
    at_up, at_dn, at_opp = (up, here), (dn, here), (opp, here)
    at_nx, at_pv = (me, nx), (me, pv)
    scale = HD ** -0.5

    def lanes(g, width=HD):
        return pl.ds(pl.multiple_of(g * width, width), width)

    def load(i):
        src, dst = ((q_hbm, q_buf), (d_hbm, d_buf), (o_hbm, o_buf), (lse_hbm, lse_buf))[i]
        return pltpu.make_async_copy(src, dst, load_sem.at[i])

    def load_kv(which, g):
        src = (k_hbm, v_hbm)[which]
        return pltpu.make_async_copy(src.at[:, lanes(g)], kv.at[0, g, which, me], kv_sem.at[which, g])

    def remote(src, dst, s, r, to):
        return pltpu.make_async_remote_copy(
            src_ref=src, dst_ref=dst, send_sem=s, recv_sem=r, device_id=to, device_id_type=MESH
        )

    def send_lse(i):
        to, target = ((up, at_up), (dn, at_dn), (opp, at_opp))[i]
        return remote(lse_cut.at[to], lse_all.at[me], lse_s.at[i], lse_r.at[i], target)

    def take_lse(i):
        src = (dn, up, opp)[i]
        return remote(lse_cut.at[src], lse_all.at[src], lse_s.at[i], lse_r.at[i], at_up)

    def own(side, g, slot):
        block = kv.at[0, g, :, slot]
        return remote(block, block, own_s.at[side, g], own_r.at[side, g], (at_up, at_dn)[side])

    def fwd(side, g, slot):
        block = kv.at[0, g, side, slot]
        return remote(block, block, fwd_s.at[side, g], fwd_r.at[side, g], (at_up, at_dn)[side])

    def ctx(g):
        return remote(kv.at[0, g], kv.at[1, g], ctx_s.at[g], ctx_r.at[g], at_nx)

    def back(g):
        return remote(back_out.at[g], back_in.at[g], back_s.at[g], back_r.at[g], at_pv)

    half = cycle // 2
    is_last = lax.rem(here, half) == half - 1
    is_first = lax.rem(here, half) == 0
    side_last = lax.rem(me + jnp.where(here < half, RING - 1, 1), RING)
    side_first = lax.rem(me + jnp.where(here < half, RING - 1, 1), RING)
    at_nx_v = (jnp.where(is_last, side_last, me), nx)
    at_pv_v = (jnp.where(is_first, side_first, me), pv)

    def start_ctx(g):
        for which, to in ((0, at_nx), (1, at_nx_v)):
            remote(kv.at[0, g, which], kv.at[1, g, which], ctx_s.at[g], ctx_r.at[g], to).start()

    def start_back(g):
        for which, to in ((0, at_pv), (1, at_pv_v)):
            remote(back_out.at[g, which], back_in.at[g, which], back_s.at[g], back_r.at[g], to).start()

    def signal(target):
        pl.semaphore_signal(barrier, inc=1, device_id=target, device_id_type=MESH)

    def cut(side, g):
        return remote(
            cut_out.at[g, side], cut_in.at[g, side], cut_s.at[side, g], cut_r.at[side, g], (at_up, at_dn)[side]
        )

    def summed(side, g):
        return remote(
            sum_out.at[g, side], sum_in.at[g, side], sum_s.at[side, g], sum_r.at[side, g], (at_up, at_dn)[side]
        )

    def loop(lo, hi, body, unroll=1):
        def step(i, carry):
            body(i)
            return carry

        lax.fori_loop(lo, hi, step, 0, unroll=unroll)

    def start_kv(g):
        load_kv(0, g).start()
        load_kv(1, g).start()

    loop(0, groups, start_kv)
    for i in (3, 1, 2, 0):
        load(i).start()

    barrier = pltpu.get_barrier_semaphore()
    for target in (at_up, at_dn, at_opp, at_nx, at_pv, at_nx_v, at_pv_v):
        signal(target)

    span_q = span_ref[2 * here + me // 2]
    first_q = (me % 2) * rows
    row = lax.broadcasted_iota(jnp.int32, (span, 2 * rows), 0)
    lane = lax.broadcasted_iota(jnp.int32, (span, 2 * rows), 1)
    ahead = lax.rem(lane, rows) - row
    for a in range(2):
        least = (span_ref[2 * here + a] - span_q) * span - first_q
        bias_own[a] = jnp.where(ahead >= least, 0.0, FAR)
    bias_prev = [jnp.where(span_q > span_ref[2 * pv + a], 0.0, FAR) for a in range(2)]

    pl.semaphore_wait(barrier, 7)

    def send_own(g):
        load_kv(0, g).wait()
        load_kv(1, g).wait()
        own(0, g, me).start()
        own(1, g, me).start()

    loop(0, min(AHEAD, groups), send_own)

    load(3).wait()
    for h in range(RING):
        lse_cut[h] = lse_buf[:, h * rows : (h + 1) * rows]
    for i in range(3):
        send_lse(i).start()
    lse_all[me] = lse_cut[me]

    ones = jnp.ones((8, 2 * HD), jnp.bfloat16)

    def make_delta(h):
        prod = o_buf[:, lanes(h)].astype(jnp.float32) * d_buf[:, lanes(h)].astype(jnp.float32)
        high = prod.astype(jnp.bfloat16)
        low = (prod - high.astype(jnp.float32)).astype(jnp.bfloat16)
        delta_all[pl.ds(h, 1), :] = dot(ones, jnp.concatenate([high, low], axis=1), NT)[0:1]

    def prepare():
        load(1).wait()
        load(2).wait()
        loop(0, groups * per, make_delta, 8)
        load(0).wait()
        for i in range(3):
            take_lse(i).wait_recv()


    def compute(g):

        def rows_of(j):
            head = g * per + 2 * j
            q_one, d_one = q_buf[:, lanes(head // 2, 2 * HD)], d_buf[:, lanes(head // 2, 2 * HD)]
            q2 = jnp.concatenate([q_one[:, :HD], q_one[:, HD:]], axis=0)
            d2 = jnp.concatenate([d_one[:, :HD], d_one[:, HD:]], axis=0)
            owner, low = head // heads_in, lax.rem(head, heads_in)
            lse2 = jnp.concatenate(
                [lse_all[owner, pl.ds(low, 1), :], lse_all[owner, pl.ds(low + 1, 1), :]], axis=1
            ) * LOG2E
            delta2 = jnp.concatenate([delta_all[pl.ds(head, 1), :], delta_all[pl.ds(head + 1, 1), :]], axis=1)
            return head, q2, d2, lse2, delta2

        for b in range(2):
            key_t[b] = kv[b, g, 0].reshape(2 * span, HD).T

        def pair(j):
            head, q2, d2, lse2, delta2 = rows_of(j)
            q_t, d_t = q2.T, d2.T
            q_all[pl.ds(pl.multiple_of(j * 2 * rows, 2 * rows), 2 * rows), :] = q2
            d_all[pl.ds(pl.multiple_of(j * 2 * rows, 2 * rows), 2 * rows), :] = d2
            for b in range(2):
                for a in range(2):
                    key = kv[b, g, 0, 2 * a : 2 * a + 2].reshape(span, HD)
                    value = kv[b, g, 1, 2 * a : 2 * a + 2].reshape(span, HD)
                    scores = dot(key, q_t, NN) * (scale * LOG2E)
                    if b == 0:
                        scores = scores - lse2 - bias_own[a]
                    else:
                        scores = scores - (lse2 + bias_prev[a])
                    probs = jnp.exp2(scores)
                    grad_probs = dot(value, d_t, NN)
                    grad_scores = (probs * (grad_probs - delta2) * scale).astype(jnp.bfloat16)
                    p_all[b, a * span : (a + 1) * span, lanes(j, 2 * HD)] = probs.astype(jnp.bfloat16)
                    s_all[b, a * span : (a + 1) * span, lanes(j, 2 * HD)] = grad_scores

        loop(0, per // 2, pair, True)
        for b in range(2):
            grad[g, b, 0] = dot(s_all[b], q_all[...], NN).reshape(RING, rows, HD)
            grad[g, b, 1] = dot(p_all[b], d_all[...], NN).reshape(RING, rows, HD)
        dq_all = dot(key_t[0], s_all[0], NN) + dot(key_t[1], s_all[1], NN)
        dq_buf[:, lanes(g, per * HD)] = jnp.concatenate([dq_all[:, rows * x : rows * (x + 1)].T for x in range(per)], axis=1).astype(jnp.bfloat16)
        back_out[g] = grad[g, 1].astype(jnp.bfloat16)

    def total(g, which, slot):
        return grad[g, 0, which, slot] + back_in[g, which, slot].astype(jnp.float32)

    def stage(i, lag, work):
        @pl.when((i >= lag) & (i < groups + lag))
        def _():
            work(i - lag)

    def forward(g):
        own(0, g, dn).wait_recv()
        fwd(0, g, dn).start()
        own(1, g, up).wait_recv()
        fwd(1, g, up).start()

    def pass_on(g):
        fwd(0, g, opp).wait_recv()
        fwd(1, g, opp).wait_recv()
        start_ctx(g)

    def start_cut(g):
        back(g).wait_recv()
        cut_out[g, 0, 0] = total(g, 0, opp).astype(jnp.bfloat16)
        cut_out[g, 0, 1] = total(g, 1, up).astype(jnp.bfloat16)
        cut(0, g).start()
        cut_out[g, 1, 0] = total(g, 1, opp).astype(jnp.bfloat16)
        cut_out[g, 1, 1] = total(g, 0, dn).astype(jnp.bfloat16)
        cut(1, g).start()

    def start_sum(g):
        cut(0, g).wait_recv()
        sum_out[g, 0] = (total(g, 0, up) + cut_in[g, 0, 0].astype(jnp.float32)).astype(jnp.bfloat16)
        summed(0, g).start()
        cut(1, g).wait_recv()
        sum_out[g, 1] = (total(g, 1, dn) + cut_in[g, 1, 0].astype(jnp.float32)).astype(jnp.bfloat16)
        summed(1, g).start()

    def work(g):
        ctx(g).wait_recv()
        compute(g)
        start_back(g)

    def finish(g):
        summed(0, g).wait_recv()
        summed(1, g).wait_recv()
        for which, out in ((0, dk_buf), (1, dv_buf)):
            out[:, lanes(g)] = (
                total(g, which, me)
                + sum_in[g, which].astype(jnp.float32)
                + cut_in[g, 1 - which, 1].astype(jnp.float32)
            ).astype(jnp.bfloat16)

    def step(i):
        @pl.when(i < groups - AHEAD)
        def _():
            send_own(i + AHEAD)

        stage(i, 0, forward)
        stage(i, LAGS[0], pass_on)
        @pl.when(i == 1)
        def _():
            prepare()

        stage(i, LAGS[2], start_cut)
        stage(i, LAGS[3], start_sum)
        stage(i, LAGS[1], work)
        stage(i, LAGS[4], finish)

    loop(0, groups + LAGS[4], step)

    def drain(g):
        for side in range(2):
            own(side, g, me).wait_send()
            fwd(side, g, (dn, up)[side]).wait_send()
            cut(side, g).wait_send()
            summed(side, g).wait_send()
        ctx(g).wait_send()
        back(g).wait_send()

    loop(0, groups, drain)
    for i in range(3):
        send_lse(i).wait_send()


def body(query, key, value, out, dout, lse, span_order):
    rows, width = query.shape
    groups = key.shape[1] // HD
    per = width // key.shape[1]
    bf, f32 = jnp.bfloat16, jnp.float32
    dma = pltpu.SemaphoreType.DMA
    hbm = pl.BlockSpec(memory_space=pl.ANY)
    pairs = [dma((2, groups))] * 2
    ones = [dma((groups,))] * 2
    return pl.pallas_call(
        functools.partial(kernel, groups, per),
        out_shape=tuple(pltpu.VMEM(x.shape, bf) for x in (query, key, value)),
        in_specs=[hbm] * 6 + [pl.BlockSpec(memory_space=pltpu.SMEM)],
        out_specs=[pl.BlockSpec(memory_space=pltpu.VMEM)] * 3,
        scratch_shapes=[
            pltpu.VMEM(query.shape, bf),
            pltpu.VMEM(query.shape, bf),
            pltpu.VMEM(query.shape, bf),
            pltpu.VMEM(lse.shape[::-1], f32),
            pltpu.VMEM((RING, lse.shape[1], rows), f32),
            pltpu.VMEM((RING, lse.shape[1], rows), f32),
            pltpu.VMEM((groups * per, rows), f32),
            pltpu.VMEM((2, 2 * rows, 2 * rows), f32),
            pltpu.VMEM((2, groups, 2, RING, rows, HD), bf),
            pltpu.VMEM((groups, 2, 2, RING, rows, HD), f32),
            pltpu.VMEM((groups, 2, RING, rows, HD), bf),
            pltpu.VMEM((groups, 2, RING, rows, HD), bf),
            pltpu.VMEM((groups, 2, 2, rows, HD), bf),
            pltpu.VMEM((groups, 2, 2, rows, HD), bf),
            pltpu.VMEM((groups, 2, rows, HD), bf),
            pltpu.VMEM((groups, 2, rows, HD), bf),
            pltpu.VMEM((2, HD, RING * rows), bf),
            pltpu.VMEM((2, RING * rows, per * rows), bf),
            pltpu.VMEM((2, RING * rows, per * rows), bf),
            pltpu.VMEM((per * rows, HD), bf),
            pltpu.VMEM((per * rows, HD), bf),
            dma((4,)),
            dma((2, groups)),
            dma((3,)),
            dma((3,)),
            *pairs,
            *pairs,
            *ones,
            *ones,
            *pairs,
            *pairs,
        ],
        compiler_params=pltpu.CompilerParams(
            collective_id=0, has_side_effects=True, vmem_limit_bytes=56 * 1024 * 1024
        ),
        cost_estimate=pl.CostEstimate(
            flops=20 * rows * width * RING * rows, bytes_accessed=10 * rows * width, transcendentals=0
        ),
    )(query, key, value, out, dout, lse.T, span_order)


def solution(mesh):
    token = P(("ctx", "head"), None)
    return jax.shard_map(
        body,
        mesh=mesh,
        in_specs=(token, token, token, token, token, P("ctx", "head"), P()),
        out_specs=(token, token, token),
        check_vma=False,
    )
```

```python
import functools
import math

import jax
import jax.numpy as jnp
from jax import lax
from jax.experimental import pallas as pl
from jax.experimental.pallas import tpu as pltpu
from jax.sharding import PartitionSpec as P

HD = 128
RING = 4
LOG2E = math.log2(math.e)
FAR = 1e30
AHEAD = 2
LAGS = (1, 3, 5, 7, 9)
MESH = pl.DeviceIdType.MESH
NT = (((1,), (1,)), ((), ()))
NN = (((1,), (0,)), ((), ()))


def dot(a, b, dims):
    return lax.dot_general(a, b, dims, preferred_element_type=jnp.float32)


def kernel(
    groups, per, q_hbm, k_hbm, v_hbm, o_hbm, d_hbm, lse_hbm, span_ref,
    dq_buf, dk_buf, dv_buf,
    q_buf, d_buf, o_buf, lse_buf, lse_cut, lse_all, delta_all, bias_own,
    kv, grad, back_out, back_in, cut_out, cut_in, sum_out, sum_in,
    key_t, p_all, s_all, q_all, d_all,
    load_sem, kv_sem,
    lse_s, lse_r, own_s, own_r, fwd_s, fwd_r, ctx_s, ctx_r, back_s, back_r, cut_s, cut_r, sum_s, sum_r,
):
    rows = q_buf.shape[0]
    span = 2 * rows
    heads_in = lse_cut.shape[1]
    cycle = lax.axis_size("ctx")
    me = lax.axis_index("head")
    here = lax.axis_index("ctx")
    up, opp, dn = lax.rem(me + 1, RING), lax.rem(me + 2, RING), lax.rem(me + 3, RING)
    nx, pv = lax.rem(here + 1, cycle), lax.rem(here + cycle - 1, cycle)
    at_up, at_dn, at_opp = (up, here), (dn, here), (opp, here)
    at_nx, at_pv = (me, nx), (me, pv)
    scale = HD ** -0.5

    def lanes(g, width=HD):
        return pl.ds(pl.multiple_of(g * width, width), width)

    def load(i):
        src, dst = ((q_hbm, q_buf), (d_hbm, d_buf), (o_hbm, o_buf), (lse_hbm, lse_buf))[i]
        return pltpu.make_async_copy(src, dst, load_sem.at[i])

    def load_kv(which, g):
        src = (k_hbm, v_hbm)[which]
        return pltpu.make_async_copy(src.at[:, lanes(g)], kv.at[0, g, which, me], kv_sem.at[which, g])

    def remote(src, dst, s, r, to):
        return pltpu.make_async_remote_copy(
            src_ref=src, dst_ref=dst, send_sem=s, recv_sem=r, device_id=to, device_id_type=MESH
        )

    def send_lse(i):
        to, target = ((up, at_up), (dn, at_dn), (opp, at_opp))[i]
        return remote(lse_cut.at[to], lse_all.at[me], lse_s.at[i], lse_r.at[i], target)

    def take_lse(i):
        src = (dn, up, opp)[i]
        return remote(lse_cut.at[src], lse_all.at[src], lse_s.at[i], lse_r.at[i], at_up)

    def own(side, g, slot):
        block = kv.at[0, g, :, slot]
        return remote(block, block, own_s.at[side, g], own_r.at[side, g], (at_up, at_dn)[side])

    def fwd(side, g, slot):
        block = kv.at[0, g, side, slot]
        return remote(block, block, fwd_s.at[side, g], fwd_r.at[side, g], (at_up, at_dn)[side])

    def ctx(g):
        return remote(kv.at[0, g], kv.at[1, g], ctx_s.at[g], ctx_r.at[g], at_nx)

    def back(g):
        return remote(back_out.at[g], back_in.at[g], back_s.at[g], back_r.at[g], at_pv)

    half = cycle // 2
    is_last = lax.rem(here, half) == half - 1
    is_first = lax.rem(here, half) == 0
    side_last = lax.rem(me + jnp.where(here < half, RING - 1, 1), RING)
    side_first = lax.rem(me + jnp.where(here < half, RING - 1, 1), RING)
    at_nx_v = (jnp.where(is_last, side_last, me), nx)
    at_pv_v = (jnp.where(is_first, side_first, me), pv)

    def start_ctx(g):
        for which, to in ((0, at_nx), (1, at_nx_v)):
            remote(kv.at[0, g, which], kv.at[1, g, which], ctx_s.at[g], ctx_r.at[g], to).start()

    def start_back(g):
        for which, to in ((0, at_pv), (1, at_pv_v)):
            remote(back_out.at[g, which], back_in.at[g, which], back_s.at[g], back_r.at[g], to).start()

    def signal(target):
        pl.semaphore_signal(barrier, inc=1, device_id=target, device_id_type=MESH)

    def cut(side, g):
        return remote(
            cut_out.at[g, side], cut_in.at[g, side], cut_s.at[side, g], cut_r.at[side, g], (at_up, at_dn)[side]
        )

    def summed(side, g):
        return remote(
            sum_out.at[g, side], sum_in.at[g, side], sum_s.at[side, g], sum_r.at[side, g], (at_up, at_dn)[side]
        )

    def loop(lo, hi, body, unroll=1):
        def step(i, carry):
            body(i)
            return carry

        lax.fori_loop(lo, hi, step, 0, unroll=unroll)

    def start_kv(g):
        load_kv(0, g).start()
        load_kv(1, g).start()

    loop(0, groups, start_kv)
    for i in (3, 1, 2, 0):
        load(i).start()

    barrier = pltpu.get_barrier_semaphore()
    for target in (at_up, at_dn, at_opp, at_nx, at_pv, at_nx_v, at_pv_v):
        signal(target)

    span_q = span_ref[2 * here + me // 2]
    first_q = (me % 2) * rows
    row = lax.broadcasted_iota(jnp.int32, (span, 2 * rows), 0)
    lane = lax.broadcasted_iota(jnp.int32, (span, 2 * rows), 1)
    ahead = lax.rem(lane, rows) - row
    for a in range(2):
        least = (span_ref[2 * here + a] - span_q) * span - first_q
        bias_own[a] = jnp.where(ahead >= least, 0.0, FAR)
    bias_prev = [jnp.where(span_q > span_ref[2 * pv + a], 0.0, FAR) for a in range(2)]

    pl.semaphore_wait(barrier, 7)

    def send_own(g):
        load_kv(0, g).wait()
        load_kv(1, g).wait()
        own(0, g, me).start()
        own(1, g, me).start()

    loop(0, min(AHEAD, groups), send_own)

    load(3).wait()
    for h in range(RING):
        lse_cut[h] = lse_buf[:, h * rows : (h + 1) * rows]
    for i in range(3):
        send_lse(i).start()
    lse_all[me] = lse_cut[me]

    ones = jnp.ones((8, 2 * HD), jnp.bfloat16)

    def make_delta(h):
        prod = o_buf[:, lanes(h)].astype(jnp.float32) * d_buf[:, lanes(h)].astype(jnp.float32)
        high = prod.astype(jnp.bfloat16)
        low = (prod - high.astype(jnp.float32)).astype(jnp.bfloat16)
        delta_all[pl.ds(h, 1), :] = dot(ones, jnp.concatenate([high, low], axis=1), NT)[0:1]

    def prepare():
        load(1).wait()
        load(2).wait()
        loop(0, groups * per, make_delta, 8)
        load(0).wait()
        for i in range(3):
            take_lse(i).wait_recv()


    def compute(g):

        def rows_of(j):
            head = g * per + 2 * j
            q_one, d_one = q_buf[:, lanes(head // 2, 2 * HD)], d_buf[:, lanes(head // 2, 2 * HD)]
            q2 = jnp.concatenate([q_one[:, :HD], q_one[:, HD:]], axis=0)
            d2 = jnp.concatenate([d_one[:, :HD], d_one[:, HD:]], axis=0)
            owner, low = head // heads_in, lax.rem(head, heads_in)
            lse2 = jnp.concatenate(
                [lse_all[owner, pl.ds(low, 1), :], lse_all[owner, pl.ds(low + 1, 1), :]], axis=1
            ) * LOG2E
            delta2 = jnp.concatenate([delta_all[pl.ds(head, 1), :], delta_all[pl.ds(head + 1, 1), :]], axis=1)
            return head, q2, d2, lse2, delta2

        for b in range(2):
            key_t[b] = kv[b, g, 0].reshape(2 * span, HD).T

        def pair(j):
            head, q2, d2, lse2, delta2 = rows_of(j)
            q_t, d_t = q2.T, d2.T
            q_all[pl.ds(pl.multiple_of(j * 2 * rows, 2 * rows), 2 * rows), :] = q2
            d_all[pl.ds(pl.multiple_of(j * 2 * rows, 2 * rows), 2 * rows), :] = d2
            for b in range(2):
                for a in range(2):
                    key = kv[b, g, 0, 2 * a : 2 * a + 2].reshape(span, HD)
                    value = kv[b, g, 1, 2 * a : 2 * a + 2].reshape(span, HD)
                    scores = dot(key, q_t, NN) * (scale * LOG2E)
                    if b == 0:
                        scores = scores - lse2 - bias_own[a]
                    else:
                        scores = scores - (lse2 + bias_prev[a])
                    probs = jnp.exp2(scores)
                    grad_probs = dot(value, d_t, NN)
                    grad_scores = (probs * (grad_probs - delta2) * scale).astype(jnp.bfloat16)
                    p_all[b, a * span : (a + 1) * span, lanes(j, 2 * HD)] = probs.astype(jnp.bfloat16)
                    s_all[b, a * span : (a + 1) * span, lanes(j, 2 * HD)] = grad_scores

        loop(0, per // 2, pair, True)
        def keys_of(b):
            grad[g, b, 0] = dot(s_all[b], q_all[...], NN).reshape(RING, rows, HD)
            grad[g, b, 1] = dot(p_all[b], d_all[...], NN).reshape(RING, rows, HD)

        keys_of(1)
        back_out[g] = grad[g, 1].astype(jnp.bfloat16)
        start_back(g)
        keys_of(0)
        dq_all = dot(key_t[0], s_all[0], NN) + dot(key_t[1], s_all[1], NN)
        dq_buf[:, lanes(g, per * HD)] = jnp.concatenate(
            [dq_all[:, rows * x : rows * (x + 1)].T for x in range(per)], axis=1
        ).astype(jnp.bfloat16)

    def total(g, which, slot):
        return grad[g, 0, which, slot] + back_in[g, which, slot].astype(jnp.float32)

    def stage(i, lag, work):
        @pl.when((i >= lag) & (i < groups + lag))
        def _():
            work(i - lag)

    def forward(g):
        own(0, g, dn).wait_recv()
        fwd(0, g, dn).start()
        own(1, g, up).wait_recv()
        fwd(1, g, up).start()

    def pass_on(g):
        fwd(0, g, opp).wait_recv()
        fwd(1, g, opp).wait_recv()
        start_ctx(g)

    def start_cut(g):
        back(g).wait_recv()
        cut_out[g, 0, 0] = total(g, 0, opp).astype(jnp.bfloat16)
        cut_out[g, 0, 1] = total(g, 1, up).astype(jnp.bfloat16)
        cut(0, g).start()
        cut_out[g, 1, 0] = total(g, 1, opp).astype(jnp.bfloat16)
        cut_out[g, 1, 1] = total(g, 0, dn).astype(jnp.bfloat16)
        cut(1, g).start()

    def start_sum(g):
        cut(0, g).wait_recv()
        sum_out[g, 0] = (total(g, 0, up) + cut_in[g, 0, 0].astype(jnp.float32)).astype(jnp.bfloat16)
        summed(0, g).start()
        cut(1, g).wait_recv()
        sum_out[g, 1] = (total(g, 1, dn) + cut_in[g, 1, 0].astype(jnp.float32)).astype(jnp.bfloat16)
        summed(1, g).start()

    def work(g):
        ctx(g).wait_recv()
        compute(g)

    def finish(g):
        summed(0, g).wait_recv()
        summed(1, g).wait_recv()
        for which, out in ((0, dk_buf), (1, dv_buf)):
            out[:, lanes(g)] = (
                total(g, which, me)
                + sum_in[g, which].astype(jnp.float32)
                + cut_in[g, 1 - which, 1].astype(jnp.float32)
            ).astype(jnp.bfloat16)

    def step(i):
        @pl.when(i < groups - AHEAD)
        def _():
            send_own(i + AHEAD)

        stage(i, 0, forward)
        stage(i, LAGS[0], pass_on)
        @pl.when(i == 1)
        def _():
            prepare()

        stage(i, LAGS[2], start_cut)
        stage(i, LAGS[3], start_sum)
        stage(i, LAGS[1], work)
        stage(i, LAGS[4], finish)

    loop(0, groups + LAGS[4], step)

    def drain(g):
        for side in range(2):
            own(side, g, me).wait_send()
            fwd(side, g, (dn, up)[side]).wait_send()
            cut(side, g).wait_send()
            summed(side, g).wait_send()
        ctx(g).wait_send()
        back(g).wait_send()

    loop(0, groups, drain)
    for i in range(3):
        send_lse(i).wait_send()


def body(query, key, value, out, dout, lse, span_order):
    rows, width = query.shape
    groups = key.shape[1] // HD
    per = width // key.shape[1]
    bf, f32 = jnp.bfloat16, jnp.float32
    dma = pltpu.SemaphoreType.DMA
    hbm = pl.BlockSpec(memory_space=pl.ANY)
    pairs = [dma((2, groups))] * 2
    ones = [dma((groups,))] * 2
    return pl.pallas_call(
        functools.partial(kernel, groups, per),
        out_shape=tuple(pltpu.VMEM(x.shape, bf) for x in (query, key, value)),
        in_specs=[hbm] * 6 + [pl.BlockSpec(memory_space=pltpu.SMEM)],
        out_specs=[pl.BlockSpec(memory_space=pltpu.VMEM)] * 3,
        scratch_shapes=[
            pltpu.VMEM(query.shape, bf),
            pltpu.VMEM(query.shape, bf),
            pltpu.VMEM(query.shape, bf),
            pltpu.VMEM(lse.shape[::-1], f32),
            pltpu.VMEM((RING, lse.shape[1], rows), f32),
            pltpu.VMEM((RING, lse.shape[1], rows), f32),
            pltpu.VMEM((groups * per, rows), f32),
            pltpu.VMEM((2, 2 * rows, 2 * rows), f32),
            pltpu.VMEM((2, groups, 2, RING, rows, HD), bf),
            pltpu.VMEM((groups, 2, 2, RING, rows, HD), f32),
            pltpu.VMEM((groups, 2, RING, rows, HD), bf),
            pltpu.VMEM((groups, 2, RING, rows, HD), bf),
            pltpu.VMEM((groups, 2, 2, rows, HD), bf),
            pltpu.VMEM((groups, 2, 2, rows, HD), bf),
            pltpu.VMEM((groups, 2, rows, HD), bf),
            pltpu.VMEM((groups, 2, rows, HD), bf),
            pltpu.VMEM((2, HD, RING * rows), bf),
            pltpu.VMEM((2, RING * rows, per * rows), bf),
            pltpu.VMEM((2, RING * rows, per * rows), bf),
            pltpu.VMEM((per * rows, HD), bf),
            pltpu.VMEM((per * rows, HD), bf),
            dma((4,)),
            dma((2, groups)),
            dma((3,)),
            dma((3,)),
            *pairs,
            *pairs,
            *ones,
            *ones,
            *pairs,
            *pairs,
        ],
        compiler_params=pltpu.CompilerParams(
            collective_id=0, has_side_effects=True, vmem_limit_bytes=56 * 1024 * 1024
        ),
        cost_estimate=pl.CostEstimate(
            flops=20 * rows * width * RING * rows, bytes_accessed=10 * rows * width, transcendentals=0
        ),
    )(query, key, value, out, dout, lse.T, span_order)


def solution(mesh):
    token = P(("ctx", "head"), None)
    return jax.shard_map(
        body,
        mesh=mesh,
        in_specs=(token, token, token, token, token, P("ctx", "head"), P()),
        out_specs=(token, token, token),
        check_vma=False,
    )
```

```python
import functools
import math

import jax
import jax.numpy as jnp
from jax import lax
from jax.experimental import pallas as pl
from jax.experimental.pallas import tpu as pltpu
from jax.sharding import PartitionSpec as P

HD = 128
RING = 4
LOG2E = math.log2(math.e)
FAR = 1e30
AHEAD = 2
LAGS = (1, 3, 5, 7, 9)
MESH = pl.DeviceIdType.MESH
NT = (((1,), (1,)), ((), ()))
NN = (((1,), (0,)), ((), ()))


def dot(a, b, dims):
    return lax.dot_general(a, b, dims, preferred_element_type=jnp.float32)


def kernel(
    groups, per, q_hbm, k_hbm, v_hbm, o_hbm, d_hbm, lse_hbm, span_ref,
    dq_buf, dk_buf, dv_buf,
    q_buf, d_buf, o_buf, lse_buf, lse_cut, lse_all, delta_all, bias_own,
    kv, grad, back_out, back_in, cut_out, cut_in, sum_out, sum_in,
    key_t, p_all, s_all, q_all, d_all,
    load_sem, kv_sem,
    lse_s, lse_r, own_s, own_r, fwd_s, fwd_r, ctx_s, ctx_r, back_s, back_r, cut_s, cut_r, sum_s, sum_r,
):
    rows = q_buf.shape[0]
    span = 2 * rows
    heads_in = lse_cut.shape[1]
    cycle = lax.axis_size("ctx")
    me = lax.axis_index("head")
    here = lax.axis_index("ctx")
    up, opp, dn = lax.rem(me + 1, RING), lax.rem(me + 2, RING), lax.rem(me + 3, RING)
    nx, pv = lax.rem(here + 1, cycle), lax.rem(here + cycle - 1, cycle)
    at_up, at_dn, at_opp = (up, here), (dn, here), (opp, here)
    at_nx, at_pv = (me, nx), (me, pv)
    scale = HD ** -0.5

    def lanes(g, width=HD):
        return pl.ds(pl.multiple_of(g * width, width), width)

    def load(i):
        src, dst = ((q_hbm, q_buf), (d_hbm, d_buf), (o_hbm, o_buf), (lse_hbm, lse_buf))[i]
        return pltpu.make_async_copy(src, dst, load_sem.at[i])

    def load_kv(which, g):
        src = (k_hbm, v_hbm)[which]
        return pltpu.make_async_copy(src.at[:, lanes(g)], kv.at[0, g, which, me], kv_sem.at[which, g])

    def remote(src, dst, s, r, to):
        return pltpu.make_async_remote_copy(
            src_ref=src, dst_ref=dst, send_sem=s, recv_sem=r, device_id=to, device_id_type=MESH
        )

    def send_lse(i):
        to, target = ((up, at_up), (dn, at_dn), (opp, at_opp))[i]
        return remote(lse_cut.at[to], lse_all.at[me], lse_s.at[i], lse_r.at[i], target)

    def take_lse(i):
        src = (dn, up, opp)[i]
        return remote(lse_cut.at[src], lse_all.at[src], lse_s.at[i], lse_r.at[i], at_up)

    def own(side, g, slot):
        block = kv.at[0, g, :, slot]
        return remote(block, block, own_s.at[side, g], own_r.at[side, g], (at_up, at_dn)[side])

    def fwd(side, g, slot):
        block = kv.at[0, g, side, slot]
        return remote(block, block, fwd_s.at[side, g], fwd_r.at[side, g], (at_up, at_dn)[side])

    def ctx(g):
        return remote(kv.at[0, g], kv.at[1, g], ctx_s.at[g], ctx_r.at[g], at_nx)

    def back(g):
        return remote(back_out.at[g], back_in.at[g], back_s.at[g], back_r.at[g], at_pv)

    half = cycle // 2
    is_last = lax.rem(here, half) == half - 1
    is_first = lax.rem(here, half) == 0
    side_last = lax.rem(me + jnp.where(here < half, RING - 1, 1), RING)
    side_first = lax.rem(me + jnp.where(here < half, RING - 1, 1), RING)
    at_nx_v = (jnp.where(is_last, side_last, me), nx)
    at_pv_v = (jnp.where(is_first, side_first, me), pv)

    def start_ctx(g):
        for which, to in ((0, at_nx), (1, at_nx_v)):
            remote(kv.at[0, g, which], kv.at[1, g, which], ctx_s.at[g], ctx_r.at[g], to).start()

    def start_back(g):
        for which, to in ((0, at_pv), (1, at_pv_v)):
            remote(back_out.at[g, which], back_in.at[g, which], back_s.at[g], back_r.at[g], to).start()

    def signal(target):
        pl.semaphore_signal(barrier, inc=1, device_id=target, device_id_type=MESH)

    def cut(side, g):
        return remote(
            cut_out.at[g, side], cut_in.at[g, side], cut_s.at[side, g], cut_r.at[side, g], (at_up, at_dn)[side]
        )

    def summed(side, g):
        return remote(
            sum_out.at[g, side], sum_in.at[g, side], sum_s.at[side, g], sum_r.at[side, g], (at_up, at_dn)[side]
        )

    def loop(lo, hi, body, unroll=1):
        def step(i, carry):
            body(i)
            return carry

        lax.fori_loop(lo, hi, step, 0, unroll=unroll)

    def start_kv(g):
        load_kv(0, g).start()
        load_kv(1, g).start()

    loop(0, groups, start_kv)
    for i in (3, 1, 2, 0):
        load(i).start()

    barrier = pltpu.get_barrier_semaphore()
    for target in (at_up, at_dn, at_opp, at_nx, at_pv, at_nx_v, at_pv_v):
        signal(target)

    span_q = span_ref[2 * here + me // 2]
    first_q = (me % 2) * rows
    row = lax.broadcasted_iota(jnp.int32, (span, 2 * rows), 0)
    lane = lax.broadcasted_iota(jnp.int32, (span, 2 * rows), 1)
    ahead = lax.rem(lane, rows) - row
    for a in range(2):
        least = (span_ref[2 * here + a] - span_q) * span - first_q
        bias_own[a] = jnp.where(ahead >= least, 0.0, FAR)
    bias_prev = [jnp.where(span_q > span_ref[2 * pv + a], 0.0, FAR) for a in range(2)]

    pl.semaphore_wait(barrier, 7)

    def send_own(g):
        load_kv(0, g).wait()
        load_kv(1, g).wait()
        own(0, g, me).start()
        own(1, g, me).start()

    loop(0, min(AHEAD, groups), send_own)

    load(3).wait()
    for h in range(RING):
        lse_cut[h] = lse_buf[:, h * rows : (h + 1) * rows]
    for i in range(3):
        send_lse(i).start()
    lse_all[me] = lse_cut[me]

    ones = jnp.ones((8, 2 * HD), jnp.bfloat16)

    def make_delta(h):
        prod = o_buf[:, lanes(h)].astype(jnp.float32) * d_buf[:, lanes(h)].astype(jnp.float32)
        high = prod.astype(jnp.bfloat16)
        low = (prod - high.astype(jnp.float32)).astype(jnp.bfloat16)
        delta_all[pl.ds(h, 1), :] = dot(ones, jnp.concatenate([high, low], axis=1), NT)[0:1]

    load(1).wait()
    load(2).wait()
    loop(0, groups * per, make_delta, 8)

    def prepare():
        load(0).wait()
        for i in range(3):
            take_lse(i).wait_recv()


    def compute(g):

        def rows_of(j):
            head = g * per + 2 * j
            q_one, d_one = q_buf[:, lanes(head // 2, 2 * HD)], d_buf[:, lanes(head // 2, 2 * HD)]
            q2 = jnp.concatenate([q_one[:, :HD], q_one[:, HD:]], axis=0)
            d2 = jnp.concatenate([d_one[:, :HD], d_one[:, HD:]], axis=0)
            owner, low = head // heads_in, lax.rem(head, heads_in)
            lse2 = jnp.concatenate(
                [lse_all[owner, pl.ds(low, 1), :], lse_all[owner, pl.ds(low + 1, 1), :]], axis=1
            ) * LOG2E
            delta2 = jnp.concatenate([delta_all[pl.ds(head, 1), :], delta_all[pl.ds(head + 1, 1), :]], axis=1)
            return head, q2, d2, lse2, delta2

        for b in range(2):
            key_t[b] = kv[b, g, 0].reshape(2 * span, HD).T

        def pair(j):
            head, q2, d2, lse2, delta2 = rows_of(j)
            q_t, d_t = q2.T, d2.T
            q_all[pl.ds(pl.multiple_of(j * 2 * rows, 2 * rows), 2 * rows), :] = q2
            d_all[pl.ds(pl.multiple_of(j * 2 * rows, 2 * rows), 2 * rows), :] = d2
            for b in range(2):
                for a in range(2):
                    key = kv[b, g, 0, 2 * a : 2 * a + 2].reshape(span, HD)
                    value = kv[b, g, 1, 2 * a : 2 * a + 2].reshape(span, HD)
                    scores = dot(key, q_t, NN) * (scale * LOG2E)
                    if b == 0:
                        scores = scores - lse2 - bias_own[a]
                    else:
                        scores = scores - (lse2 + bias_prev[a])
                    probs = jnp.exp2(scores)
                    grad_probs = dot(value, d_t, NN)
                    grad_scores = (probs * (grad_probs - delta2) * scale).astype(jnp.bfloat16)
                    p_all[b, a * span : (a + 1) * span, lanes(j, 2 * HD)] = probs.astype(jnp.bfloat16)
                    s_all[b, a * span : (a + 1) * span, lanes(j, 2 * HD)] = grad_scores

        loop(0, per // 2, pair, True)
        def keys_of(b):
            grad[g, b, 0] = dot(s_all[b], q_all[...], NN).reshape(RING, rows, HD)
            grad[g, b, 1] = dot(p_all[b], d_all[...], NN).reshape(RING, rows, HD)

        keys_of(1)
        back_out[g] = grad[g, 1].astype(jnp.bfloat16)
        start_back(g)
        keys_of(0)
        dq_all = dot(key_t[0], s_all[0], NN) + dot(key_t[1], s_all[1], NN)
        dq_buf[:, lanes(g, per * HD)] = jnp.concatenate(
            [dq_all[:, rows * x : rows * (x + 1)].T for x in range(per)], axis=1
        ).astype(jnp.bfloat16)

    def total(g, which, slot):
        return grad[g, 0, which, slot] + back_in[g, which, slot].astype(jnp.float32)

    def stage(i, lag, work):
        @pl.when((i >= lag) & (i < groups + lag))
        def _():
            work(i - lag)

    def forward(g):
        own(0, g, dn).wait_recv()
        fwd(0, g, dn).start()
        own(1, g, up).wait_recv()
        fwd(1, g, up).start()

    def pass_on(g):
        fwd(0, g, opp).wait_recv()
        fwd(1, g, opp).wait_recv()
        start_ctx(g)

    def start_cut(g):
        back(g).wait_recv()
        cut_out[g, 0, 0] = total(g, 0, opp).astype(jnp.bfloat16)
        cut_out[g, 0, 1] = total(g, 1, up).astype(jnp.bfloat16)
        cut(0, g).start()
        cut_out[g, 1, 0] = total(g, 1, opp).astype(jnp.bfloat16)
        cut_out[g, 1, 1] = total(g, 0, dn).astype(jnp.bfloat16)
        cut(1, g).start()

    def start_sum(g):
        cut(0, g).wait_recv()
        sum_out[g, 0] = (total(g, 0, up) + cut_in[g, 0, 0].astype(jnp.float32)).astype(jnp.bfloat16)
        summed(0, g).start()
        cut(1, g).wait_recv()
        sum_out[g, 1] = (total(g, 1, dn) + cut_in[g, 1, 0].astype(jnp.float32)).astype(jnp.bfloat16)
        summed(1, g).start()

    def work(g):
        ctx(g).wait_recv()
        compute(g)

    def finish(g):
        summed(0, g).wait_recv()
        summed(1, g).wait_recv()
        for which, out in ((0, dk_buf), (1, dv_buf)):
            out[:, lanes(g)] = (
                total(g, which, me)
                + sum_in[g, which].astype(jnp.float32)
                + cut_in[g, 1 - which, 1].astype(jnp.float32)
            ).astype(jnp.bfloat16)

    def step(i):
        @pl.when(i < groups - AHEAD)
        def _():
            send_own(i + AHEAD)

        stage(i, 0, forward)
        stage(i, LAGS[0], pass_on)
        @pl.when(i == 1)
        def _():
            prepare()

        stage(i, LAGS[2], start_cut)
        stage(i, LAGS[3], start_sum)
        stage(i, LAGS[1], work)
        stage(i, LAGS[4], finish)

    loop(0, groups + LAGS[4], step)

    def drain(g):
        for side in range(2):
            own(side, g, me).wait_send()
            fwd(side, g, (dn, up)[side]).wait_send()
            cut(side, g).wait_send()
            summed(side, g).wait_send()
        ctx(g).wait_send()
        back(g).wait_send()

    loop(0, groups, drain)
    for i in range(3):
        send_lse(i).wait_send()


def body(query, key, value, out, dout, lse, span_order):
    rows, width = query.shape
    groups = key.shape[1] // HD
    per = width // key.shape[1]
    bf, f32 = jnp.bfloat16, jnp.float32
    dma = pltpu.SemaphoreType.DMA
    hbm = pl.BlockSpec(memory_space=pl.ANY)
    pairs = [dma((2, groups))] * 2
    ones = [dma((groups,))] * 2
    return pl.pallas_call(
        functools.partial(kernel, groups, per),
        out_shape=tuple(pltpu.VMEM(x.shape, bf) for x in (query, key, value)),
        in_specs=[hbm] * 6 + [pl.BlockSpec(memory_space=pltpu.SMEM)],
        out_specs=[pl.BlockSpec(memory_space=pltpu.VMEM)] * 3,
        scratch_shapes=[
            pltpu.VMEM(query.shape, bf),
            pltpu.VMEM(query.shape, bf),
            pltpu.VMEM(query.shape, bf),
            pltpu.VMEM(lse.shape[::-1], f32),
            pltpu.VMEM((RING, lse.shape[1], rows), f32),
            pltpu.VMEM((RING, lse.shape[1], rows), f32),
            pltpu.VMEM((groups * per, rows), f32),
            pltpu.VMEM((2, 2 * rows, 2 * rows), f32),
            pltpu.VMEM((2, groups, 2, RING, rows, HD), bf),
            pltpu.VMEM((groups, 2, 2, RING, rows, HD), f32),
            pltpu.VMEM((groups, 2, RING, rows, HD), bf),
            pltpu.VMEM((groups, 2, RING, rows, HD), bf),
            pltpu.VMEM((groups, 2, 2, rows, HD), bf),
            pltpu.VMEM((groups, 2, 2, rows, HD), bf),
            pltpu.VMEM((groups, 2, rows, HD), bf),
            pltpu.VMEM((groups, 2, rows, HD), bf),
            pltpu.VMEM((2, HD, RING * rows), bf),
            pltpu.VMEM((2, RING * rows, per * rows), bf),
            pltpu.VMEM((2, RING * rows, per * rows), bf),
            pltpu.VMEM((per * rows, HD), bf),
            pltpu.VMEM((per * rows, HD), bf),
            dma((4,)),
            dma((2, groups)),
            dma((3,)),
            dma((3,)),
            *pairs,
            *pairs,
            *ones,
            *ones,
            *pairs,
            *pairs,
        ],
        compiler_params=pltpu.CompilerParams(
            collective_id=0, has_side_effects=True, vmem_limit_bytes=56 * 1024 * 1024
        ),
        cost_estimate=pl.CostEstimate(
            flops=20 * rows * width * RING * rows, bytes_accessed=10 * rows * width, transcendentals=0
        ),
    )(query, key, value, out, dout, lse.T, span_order)


def solution(mesh):
    token = P(("ctx", "head"), None)
    return jax.shard_map(
        body,
        mesh=mesh,
        in_specs=(token, token, token, token, token, P("ctx", "head"), P()),
        out_specs=(token, token, token),
        check_vma=False,
    )
```
